32 devices in a mesh: groups: 2 (over y), dom: 4 (over z), ens: 2 (over x), rep: 2 (over core).
Axes of the slice: x: 2, y: 2, z: 4, core: 2. Of those that a mesh axis runs over, the one named last changes fastest.
Arguments:
- grid_h: float32 [4, 8192, 512], P(('groups', 'ens'), ('dom', 'rep')), parts along dimension 0, may hold values from -6 to 6
- mesh_h: float32 [4, 1024, 512], P(('groups', 'ens'), ('dom', 'rep')), parts along dimension 0, may hold values from -6 to 6
- cotangent: float32 [4, 1024, 512], P(('groups', 'ens'), ('dom', 'rep')), parts along dimension 0, may hold values from -6 to 6
- weights: float32 [6, 512, 512], replicated, may hold values from -0.25 to 0.25
- gains: float32 [2, 512], replicated, may hold values from 0.5 to 1.5
- g2m_send: int32 [8, 8, 16], P(('dom', 'rep')), may hold values from -1 to 1023, as said below
- m2m_send: int32 [8, 8, 16], P(('dom', 'rep')), may hold values from -1 to 127, as said below
- g2m_edges: int32 [2, 13312], P(None, ('dom', 'rep')), may hold values from -1 to 1151, as said below
- m2m_edges: int32 [2, 8192], P(None, ('dom', 'rep')), may hold values from -1 to 255, as said below
Outputs:
- grad_grid: float32 [4, 8192, 512], P(('groups', 'ens'), ('dom', 'rep')), parts along dimension 0
- grad_mesh: float32 [4, 1024, 512], P(('groups', 'ens'), ('dom', 'rep')), parts along dimension 0
- grad_weights: float32 [12, 512, 512], P('groups', ('dom', 'ens', 'rep')), parts along dimension 0
- grad_gains: float32 [4, 512], P('groups', ('dom', 'ens', 'rep')), parts along dimension 0
The draws below stay inside these ranges and needn't reach their ends.
There are 2 independent parts, one for each index of `groups`. The reference program is written for one: setup_inputs(seed, part) draws one part's arguments, and reference() takes and returns one part's arrays. A program takes and returns all parts, laid end to end along the dimension named above; an argument that names none is the same for every part. Nothing has to cross between parts.
Inputs may be any that keep to these rules, and one draw needn't show every extreme that they name: `g2m_send`: send[q, b, k] is a row of band q or -1; band q fills the first slots of each row with its count, -1 after; a band sends nothing to itself; a band sends to a band not adjacent to it only in the first 2 slots; band 0 fills all 16 slots to band 1 and exactly 2 to band 8 - 1. Rows may repeat. `m2m_send`: as for g2m_send, with mesh rows. `g2m_edges`: row 0 holds senders, row 1 receivers (0 to 127, or -1). A sender at or above 1024 names a slot that the source band fills. Empty slots (receiver -1, sender 0) stand at the end of a band's slots; bands 0 and 7 have none. `m2m_edges`: as for g2m_edges, with 128 in place of 1024.
All inputs are finite; a program needn't handle non-finite values.
Results may differ from the reference program's by a relative error of at most 0.000082.
Values sent between devices are 32-bit elements; how exact they have to be, the bound alone decides.
A program may use at most 128 MiB of HBM per device.

```python
import jax
import jax.numpy as jnp
from jax import lax

D = 512
G_DEV = 1024
M_DEV = 128
MEMBERS = 2
BANDS = 8
GRID = 8192
MESH = 1024
HALO = 16
FAR = 2
EG_DEV = 1664
EM_DEV = 1024


def graph_draw(key, salt_value, local_rows, target_rows, slot_count):
    key = jax.random.fold_in(key, salt_value)
    key_list = jax.random.split(key, 9)
    band_count = BANDS
    halo_rows = HALO
    far_rows = FAR
    source_index = jnp.arange(band_count, dtype=jnp.int32)[:, None]
    dest_index = jnp.arange(band_count, dtype=jnp.int32)[None, :]
    near_count = jax.random.randint(key_list[0], (band_count, band_count), halo_rows // 2, halo_rows + 1, dtype=jnp.int32)
    far_count = jax.random.randint(key_list[1], (band_count, band_count), 0, far_rows + 1, dtype=jnp.int32)
    band_gap = jnp.abs(source_index - dest_index)
    row_count = jnp.where(band_gap == 1, near_count, jnp.where(band_gap == 0, 0, far_count))
    row_count = row_count.at[0, 1].set(halo_rows).at[0, band_count - 1].set(far_rows)
    picked = jax.random.randint(key_list[2], (band_count, band_count, halo_rows), 0, local_rows, dtype=jnp.int32)
    slot_index = jnp.arange(halo_rows, dtype=jnp.int32)[None, None, :]
    send_rows = jnp.where(slot_index < row_count[:, :, None], picked, -1)
    shape_edges = (band_count, slot_count)
    band_here = jnp.broadcast_to(jnp.arange(band_count, dtype=jnp.int32)[:, None], shape_edges)
    which_kind = jax.random.randint(key_list[3], shape_edges, 0, 8, dtype=jnp.int32)
    random_band = jax.random.randint(key_list[4], shape_edges, 0, band_count, dtype=jnp.int32)
    source_band = jnp.where(which_kind == 0, band_here - 1, jnp.where(which_kind == 1, band_here + 1, random_band))
    inside = (source_band >= 0) & (source_band < band_count) & (which_kind < 3)
    safe_band = jnp.clip(source_band, 0, band_count - 1)
    have_rows = row_count[safe_band, band_here]
    inside = inside & (have_rows > 0)
    slot_row = jax.random.randint(key_list[5], shape_edges, 0, 1 << 20, dtype=jnp.int32) % jnp.maximum(have_rows, 1)
    local_pick = jax.random.randint(key_list[6], shape_edges, 0, local_rows, dtype=jnp.int32)
    senders = jnp.where(inside, local_rows + safe_band * halo_rows + slot_row, local_pick)
    receivers = jax.random.randint(key_list[7], shape_edges, 0, target_rows, dtype=jnp.int32)
    pad_count = jax.random.randint(key_list[8], (band_count,), 0, slot_count // 8 + 1, dtype=jnp.int32)
    pad_count = pad_count.at[0].set(0).at[band_count - 1].set(0)
    live_slot = jnp.arange(slot_count, dtype=jnp.int32)[None, :] < (slot_count - pad_count)[:, None]
    senders = jnp.where(live_slot, senders, 0)
    receivers = jnp.where(live_slot, receivers, -1)
    edge_lists = jnp.stack([senders.reshape(-1), receivers.reshape(-1)])
    return (send_rows, edge_lists)


def draw_g2m_send(key, part):
    return graph_draw(key, 5, G_DEV, M_DEV, EG_DEV)[0]


def draw_g2m_edges(key, part):
    return graph_draw(key, 5, G_DEV, M_DEV, EG_DEV)[1]


def draw_m2m_send(key, part):
    return graph_draw(key, 6, M_DEV, M_DEV, EM_DEV)[0]


def draw_m2m_edges(key, part):
    return graph_draw(key, 6, M_DEV, M_DEV, EM_DEV)[1]


def block_levels(key, shape, pieces, low, high):
    def one(position, shards_of):
        heights = jax.random.uniform(jax.random.fold_in(jax.random.fold_in(key, 6), position), (shards_of,), jnp.float32, low / len(pieces), high / len(pieces))
        return jnp.repeat(jnp.exp(heights), shape[position] // shards_of).reshape((-1,) + (1,) * (len(shape) - position - 1))

    level = one(*pieces[0])
    for cut in pieces[1:]:
        level = level * one(*cut)
    return level


def gaussian(key, shape, spread, bound, shards=(), kind=jnp.bfloat16):
    entries = spread * jax.random.normal(key, shape, jnp.float32)
    if shards:
        entries = entries * block_levels(key, shape, shards, -0.22, 0.18)
    return jnp.clip(entries, -bound, bound).astype(kind)


def setup_inputs(seed: int = 0, part: int = 0) -> dict:
    key_of = jax.random.split(jax.random.key(seed), 10)
    part_keys = jax.random.split(jax.random.fold_in(key_of[9], part), 10)
    grid_h = gaussian(part_keys[0], (MEMBERS, GRID, D), 1.0, 6.0, ((0, 2), (1, 8)), jnp.float32)
    mesh_h = gaussian(part_keys[1], (MEMBERS, MESH, D), 1.0, 6.0, ((0, 2), (1, 8)), jnp.float32)
    cotangent = gaussian(part_keys[2], (MEMBERS, MESH, D), 1.0, 6.0, ((0, 2), (1, 8)), jnp.float32)
    weights = gaussian(key_of[3], (6, D, D), D ** -0.5, 0.25, (), jnp.float32)
    gains = jnp.clip(jax.random.uniform(key_of[4], (2, D), jnp.float32, 0.5, 1.5), 0.5, 1.5)
    g2m_send = draw_g2m_send(jax.random.fold_in(key_of[9], 71), part)
    m2m_send = draw_m2m_send(jax.random.fold_in(key_of[9], 71), part)
    g2m_edges = draw_g2m_edges(jax.random.fold_in(key_of[9], 71), part)
    m2m_edges = draw_m2m_edges(jax.random.fold_in(key_of[9], 71), part)
    return dict(grid_h=grid_h, mesh_h=mesh_h, cotangent=cotangent, weights=weights, gains=gains, g2m_send=g2m_send, m2m_send=m2m_send, g2m_edges=g2m_edges, m2m_edges=m2m_edges)


def product(left, right):
    return jnp.matmul(left, right, precision=lax.Precision.HIGHEST, preferred_element_type=jnp.float32)

def layer_norm(values, gain_row):
    centre_mean = lax.optimization_barrier(jnp.mean(values, axis=-1, keepdims=True))
    centred = values - centre_mean
    variance = lax.optimization_barrier(jnp.mean(centred * centred, axis=-1, keepdims=True))
    return centred * lax.rsqrt(variance + 1e-05) * gain_row

def global_ends(edge_lists, send_rows, local_rows, target_rows):
    band_count = send_rows.shape[0]
    halo_rows = send_rows.shape[2]
    per_band = edge_lists.shape[1] // band_count
    edge_band = (jnp.arange(edge_lists.shape[1]) // per_band).astype(jnp.int32)
    senders = edge_lists[0]
    slot_pos = jnp.maximum(senders - local_rows, 0)
    source_band = (slot_pos // halo_rows).astype(jnp.int32)
    slot_row = (slot_pos % halo_rows).astype(jnp.int32)
    remote_row = send_rows[source_band, edge_band, slot_row]
    global_send = jnp.where(senders < local_rows, edge_band * local_rows + senders, source_band * local_rows + remote_row)
    receivers = edge_lists[1]
    global_recv = jnp.where(receivers >= 0, edge_band * target_rows + receivers, band_count * target_rows)
    return (global_send.astype(jnp.int32), global_recv.astype(jnp.int32))

def edge_section(source_proj, target, w_recv, w_out, gain_row, global_send, global_recv):
    total_rows = target.shape[0]
    recv_proj = product(target, w_recv)
    pre_act = source_proj[global_send] + recv_proj[jnp.minimum(global_recv, total_rows - 1)]
    message = product(jax.nn.silu(pre_act), w_out)
    gathered = jax.ops.segment_sum(message, global_recv, num_segments=total_rows + 1)[:total_rows]
    return target + layer_norm(gathered, gain_row)

def reference(grid_h, mesh_h, cotangent, weights, gains, g2m_send, m2m_send, g2m_edges, m2m_edges):
    grid_send, grid_recv = global_ends(g2m_edges, g2m_send, G_DEV, M_DEV)
    mesh_send, mesh_recv = global_ends(m2m_edges, m2m_send, M_DEV, M_DEV)

    def forward(grid_rows, mesh_rows, weight_set, gain_set):
        mesh_mid = edge_section(product(grid_rows, weight_set[0]), mesh_rows, weight_set[1], weight_set[2], gain_set[0], grid_send, grid_recv)
        return edge_section(product(mesh_mid, weight_set[3]), mesh_mid, weight_set[4], weight_set[5], gain_set[1], mesh_send, mesh_recv)

    def member(member_args):
        grid_rows, mesh_rows, member_cot = member_args
        unused_out, pull_back = jax.vjp(forward, grid_rows, mesh_rows, weights, gains)
        return pull_back(member_cot)
    grad_grid, grad_mesh, weight_terms, gain_terms = lax.map(member, (grid_h, mesh_h, cotangent))
    return (grad_grid, grad_mesh, lax.optimization_barrier(jnp.sum(weight_terms, axis=0)), lax.optimization_barrier(jnp.sum(gain_terms, axis=0)))
```

```python
import functools

import jax
import jax.numpy as jnp
from jax import lax
from jax.experimental import pallas as pl
from jax.experimental.pallas import tpu as pltpu
from jax.sharding import PartitionSpec as P

F32 = jnp.float32
BF16 = jnp.bfloat16
MESH = pl.DeviceIdType.MESH

GS, GR, G2, PS, PR, P2 = range(6)


def split(x):
    hi = x.astype(BF16)
    return hi, (x - hi.astype(F32)).astype(BF16)


def dot(a, b, ca, cb):
    return lax.dot_general(a, b, (((ca,), (cb,)), ((), ())), preferred_element_type=F32)


def dot3(a, b, ca=1, cb=0):
    return dot(a[0], b[0], ca, cb) + (dot(a[0], b[1], ca, cb) + dot(a[1], b[0], ca, cb))


def dot2(sel, b, ca=1, cb=0):
    return dot(sel, b[0], ca, cb) + dot(sel, b[1], ca, cb)


def ones(mask):
    return jnp.where(mask, 1.0, 0.0).astype(BF16)


def tile_of(n, largest, unit=128):
    return max(t for t in range(unit, largest + 1, unit) if n % t == 0)


def loop(n, tile, fn):
    if n == tile:
        fn(0)
        return

    def step(i, carry):
        fn(pl.multiple_of(i * tile, tile))
        return carry

    lax.fori_loop(0, n // tile, step, 0)


def norm_stats(agg):
    mean = jnp.mean(agg, axis=-1, keepdims=True)
    cen = agg - mean
    rstd = lax.rsqrt(jnp.mean(cen * cen, axis=-1, keepdims=True) + 1e-05)
    return cen * rstd, rstd


def norm_back(d_out, unit, rstd, gain):
    d_unit = d_out * gain
    m1 = jnp.mean(d_unit, axis=-1, keepdims=True)
    m2 = jnp.mean(d_unit * unit, axis=-1, keepdims=True)
    return rstd * (d_unit - m1 - unit * m2), jnp.sum(d_out * unit, axis=0, keepdims=True)


def kernel(
    cfg,
    grid_in, mesh_in, cot_in, w_in, gains_in, gsend_in, msend_in, gedge_in, medge_in,
    *refs,
):
    bands, nx, nz, fused = cfg["bands"], cfg["nx"], cfg["nz"], cfg["fused"]
    refs = list(refs)
    out_grid, out_mesh, out_w, out_gain = refs[:4]
    refs = refs[4:]
    take = lambda: refs.pop(0)
    grid_v, w_v, wh, wl, gh, gl = take(), take(), take(), take(), take(), take()
    th, tl, col_s, col_r, act_d, eh, el = (take() for _ in range(7))
    mcol_s, mcol_r, dtab = take(), take(), take()
    pick_g, pick_m = take(), take()
    send_buf, land = take(), take()
    load_sem, halo_ss, halo_rs, out_sem = take(), take(), take(), take()
    if fused:
        dw, r1, r2, r3, gain_mine, gain_land = (take() for _ in range(6))
        s1s, s1r, s2s, s2r, s3s, s3r, gss, gsr = (take() for _ in range(8))
    else:
        dw = out_w

    dom, ens, rep = lax.axis_index("dom"), lax.axis_index("ens"), lax.axis_index("rep")
    me = dom * 2 + rep
    ng, d = grid_v.shape
    nm = mesh_in.shape[1]
    ne_g, ne_m = gedge_in.shape[1], medge_in.shape[1]
    nh = bands * 16
    tg, tm = ng + nh, nm + nh
    flat = (dom * nx + ens) * 2 + rep
    n_all = nz * nx * 2

    def band_id(b):
        return {"dom": b // 2, "rep": lax.rem(b, 2)}

    def flat_id(f):
        return {"dom": f // (2 * nx), "ens": lax.rem(f // 2, nx), "rep": lax.rem(f, 2)}

    loads = [pltpu.make_async_copy(grid_in.at[0], grid_v, load_sem.at[6])]
    loads[0].start()
    w_loads = {}
    for w in (GS, GR, G2, PS, PR, P2):
        w_loads[w] = pltpu.make_async_copy(w_in.at[w], w_v.at[w], load_sem.at[w])
        w_loads[w].start()

    barrier = pltpu.get_barrier_semaphore()
    if fused:
        for o in range(1, n_all):
            pl.semaphore_signal(barrier, inc=1, device_id=flat_id(lax.rem(flat + o, n_all)), device_id_type=MESH)
    else:
        for o in range(1, bands):
            pl.semaphore_signal(barrier, inc=1, device_id=band_id(lax.rem(me + o, bands)), device_id_type=MESH)

    for ph in range(4):
        land[ph, me] = jnp.zeros((16, d), F32)
        for o in range(2, bands - 1):
            land[ph, lax.rem(me + bands - o, bands), 8:16] = jnp.zeros((8, d), F32)

    def pick_matrix(send, rows):
        s = send[0]
        wide = jnp.broadcast_to(s[:, None, :], (bands, 16, 16)).reshape(nh, 16)
        slot = lax.rem(lax.broadcasted_iota(jnp.int32, (nh, 16), 0), 16)
        lane = lax.broadcasted_iota(jnp.int32, (nh, 16), 1)
        col = jnp.sum(jnp.where(slot == lane, wide, 0).astype(F32), axis=1, keepdims=True)
        return ones(col.astype(jnp.int32) == lax.broadcasted_iota(jnp.int32, (nh, rows), 1))

    pick_g[...] = pick_matrix(gsend_in, ng)
    pick_m[...] = pick_matrix(msend_in, nm)

    def columns(edges, dst_s, dst_r, n):
        for i in range(n // 128):
            for row, dst in ((0, dst_s), (1, dst_r)):
                line = edges[row : row + 1, i * 128 : (i + 1) * 128]
                dst[i * 128 : (i + 1) * 128, :] = jnp.broadcast_to(line.astype(F32), (128, 128)).T.astype(jnp.int32)

    def exchange(ph):
        copies = []
        for o in range(1, bands):
            to = lax.rem(me + o, bands)
            rows = 16 if o in (1, bands - 1) else 8
            c = pltpu.make_async_remote_copy(
                src_ref=send_buf.at[ph, to, 0:rows],
                dst_ref=land.at[ph, me, 0:rows],
                send_sem=halo_ss.at[ph, o],
                recv_sem=halo_rs.at[ph, o],
                device_id=band_id(to),
                device_id_type=MESH,
            )
            c.start()
            copies.append(c)
        return copies

    sends = []

    def arrived(copies):
        for c in copies:
            c.wait_recv()
        sends.extend(copies)

    loads[0].wait()

    def split_grid(r):
        hi, lo = split(grid_v[pl.ds(r, 256), :])
        gh[pl.ds(r, 256), :] = hi
        gl[pl.ds(r, 256), :] = lo

    loop(ng, 256, split_grid)
    send_buf[0] = dot2(pick_g[...], (gh[0:ng, :], gl[0:ng, :])).reshape(bands, 16, d)
    pl.semaphore_wait(barrier, (n_all if fused else bands) - 1)
    halo = exchange(0)

    def load_w(w):
        w_loads[w].wait()
        hi, lo = split(w_v[w])
        wh[w] = hi
        wl[w] = lo

    def wt(w):
        return wh[w], wl[w]

    def put_table(r, value):
        hi, lo = split(value)
        n = value.shape[0]
        th[pl.ds(r, n), :] = hi
        tl[pl.ds(r, n), :] = lo

    load_w(GS)

    def project(r):
        put_table(r, dot3((gh[pl.ds(r, 256), :], gl[pl.ds(r, 256), :]), wt(GS)))

    loop(ng, 256, project)
    load_w(GR)
    mesh = mesh_in[0]
    mesh_s = split(mesh)
    put_table(tg, dot3(mesh_s, wt(GR)))
    columns(gedge_in, col_s, col_r, ne_g)
    columns(medge_in, mcol_s, mcol_r, ne_m)
    load_w(G2)
    load_w(PS)
    load_w(PR)
    load_w(P2)
    arrived(halo)
    hi, lo = split(land[0].reshape(nh, d))
    gh[ng:tg, :] = hi
    gl[ng:tg, :] = lo
    put_table(ng, dot3((hi, lo), wt(GS)))

    def gather(cs, cr, ne, table, tile, act):
        total = table + nm

        def step(r):
            s = cs[pl.ds(r, tile), :]
            t = cr[pl.ds(r, tile), :]
            lane = lax.broadcasted_iota(jnp.int32, (tile, 128), 1)
            parts = [ones(s == lane + j * 128) for j in range(table // 128)] + [ones(t == lane)]
            sel = jnp.concatenate(parts, axis=1)
            pre = dot2(sel, (th[0:total, :], tl[0:total, :]))
            sig = jax.nn.sigmoid(pre)
            hidden = pre * sig
            act[pl.ds(r, tile), :] = sig + hidden * (1.0 - sig)
            h, l = split(hidden)
            eh[pl.ds(r, tile), :] = h
            el[pl.ds(r, tile), :] = l

        loop(ne, tile, step)

    def incidence(edges, ne):
        return ones(edges[1:2, :] == lax.broadcasted_iota(jnp.int32, (nm, ne), 0))

    def back(cr, ne, tile, act, ds):
        def step(r):
            sel = ones(cr[pl.ds(r, tile), :] == lax.broadcasted_iota(jnp.int32, (tile, 128), 1))
            h, l = split(dot2(sel, ds) * act[pl.ds(r, tile), :])
            eh[pl.ds(r, tile), :] = h
            el[pl.ds(r, tile), :] = l

        loop(ne, tile, step)

    def scatter(edges, ne, first, n, tile):
        def step(r):
            node = lax.broadcasted_iota(jnp.int32, (tile, ne), 0) + (first + r)
            dtab[pl.ds(first + r, tile), :] = dot2(ones(edges[0:1, :] == node), (eh[0:ne, :], el[0:ne, :]))

        loop(n, tile, step)

    def store_dw(w, a, b):
        for t in range(4):
            cols = slice(t * 128, (t + 1) * 128)
            dw[w, t] = dot3((a[0][:, cols], a[1][:, cols]), b, 0, 0).reshape(dw.shape[2:])

    rs_pending = {}

    def rs1(w):
        if not fused:
            return
        c = pltpu.make_async_remote_copy(
            src_ref=dw.at[w, :, :, 1 - rep], dst_ref=r1.at[w], send_sem=s1s.at[w], recv_sem=s1r.at[w],
            device_id={"rep": 1 - rep}, device_id_type=MESH,
        )
        c.start()
        rs_pending[1, w] = [c]

    def rs2(w):
        if not fused:
            return
        arrived(rs_pending[1, w])
        r1[w] = r1[w] + dw[w, :, :, rep]
        rs_pending[2, w] = []
        for o in range(1, nx):
            to = lax.rem(ens + o, nx)
            c = pltpu.make_async_remote_copy(
                src_ref=r1.at[w, :, to], dst_ref=r2.at[w, o - 1], send_sem=s2s.at[w, o - 1], recv_sem=s2r.at[w, o - 1],
                device_id={"ens": to}, device_id_type=MESH,
            )
            c.start()
            rs_pending[2, w].append(c)

    def rs3(w):
        if not fused:
            return
        arrived(rs_pending[2, w])
        total = r1[w, :, ens]
        for o in range(nx - 1):
            total = total + r2[w, o]
        r2[w, 0] = total
        rs_pending[3, w] = []
        for o in range(1, nz):
            to = lax.rem(dom + o, nz)
            c = pltpu.make_async_remote_copy(
                src_ref=r2.at[w, 0, to], dst_ref=r3.at[w, o - 1], send_sem=s3s.at[w, o - 1], recv_sem=s3r.at[w, o - 1],
                device_id={"dom": to}, device_id_type=MESH,
            )
            c.start()
            rs_pending[3, w].append(c)

    def rs4(w):
        if not fused:
            return
        arrived(rs_pending[3, w])
        total = r2[w, 0, dom]
        for o in range(nz - 1):
            total = total + r3[w, o]
        out_w[w] = total

    tile_g = ne_g // 4 if (ne_g // 4) % 16 == 0 else 128
    tile_m = tile_of(ne_m, 512)
    gather(col_s, col_r, ne_g, tg, tile_g, act_d)
    sum_g = split(dot2(incidence(gedge_in, ne_g), (eh[0:ne_g, :], el[0:ne_g, :])))
    unit_g, rstd_g = norm_stats(dot3(sum_g, wt(G2)))
    mid = mesh + unit_g * gains_in[0:1, :]
    mid_s = split(mid)

    send_buf[1] = dot2(pick_m[...], mid_s).reshape(bands, 16, d)
    halo = exchange(1)
    put_table(0, dot3(mid_s, wt(PS)))
    put_table(tm, dot3(mid_s, wt(PR)))
    arrived(halo)
    halo_s = split(land[1].reshape(nh, d))
    put_table(nm, dot3(halo_s, wt(PS)))
    act_m = dtab
    gather(mcol_s, mcol_r, ne_m, tm, tile_m, act_m)
    sum_m = split(dot2(incidence(medge_in, ne_m), (eh[0:ne_m, :], el[0:ne_m, :])))
    unit_m, rstd_m = norm_stats(dot3(sum_m, wt(P2)))

    cot = cot_in[0]
    d_agg, d_gain_p = norm_back(cot, unit_m, rstd_m, gains_in[1:2, :])
    d_agg_s = split(d_agg)
    back(mcol_r, ne_m, tile_m, act_m, split(dot3(d_agg_s, wt(P2), 1, 1)))
    scatter(medge_in, ne_m, 0, tm, tile_of(tm, 384))
    send_buf[2] = dtab[nm:tm, :].reshape(bands, 16, d)
    halo = exchange(2)
    store_dw(P2, sum_m, d_agg_s)
    rs1(P2)
    d_recv_s = split(dot2(incidence(medge_in, ne_m), (eh[0:ne_m, :], el[0:ne_m, :])))
    store_dw(PR, mid_s, d_recv_s)
    rs1(PR)
    both = [jnp.concatenate([a, b], axis=0) for a, b in zip(mid_s, halo_s)]
    store_dw(PS, both, split(dtab[0:tm, :]))
    rs1(PS)
    d_mid = cot + dot3(d_recv_s, wt(PR), 1, 1)
    rs2(P2)
    arrived(halo)
    own = dtab[0:nm, :] + dot2(pick_m[...], split(land[2].reshape(nh, d)), 0, 0)
    d_mid = d_mid + dot3(split(own), wt(PS), 1, 1)

    d_agg, d_gain_g = norm_back(d_mid, unit_g, rstd_g, gains_in[0:1, :])
    if fused:
        row = lax.broadcasted_iota(jnp.int32, (8, d), 0)
        gain_mine[...] = jnp.where(row == 0, d_gain_g, jnp.where(row == 1, d_gain_p, 0.0))
        gain_copies = []
        for o in range(1, n_all):
            c = pltpu.make_async_remote_copy(
                src_ref=gain_mine, dst_ref=gain_land.at[o - 1], send_sem=gss.at[o - 1], recv_sem=gsr.at[o - 1],
                device_id=flat_id(lax.rem(flat + o, n_all)), device_id_type=MESH,
            )
            c.start()
            gain_copies.append(c)
    else:
        out_gain[0:1, :] = d_gain_g
        out_gain[1:2, :] = d_gain_p
    d_agg_s = split(d_agg)
    store_dw(G2, sum_g, d_agg_s)
    rs1(G2)
    rs2(PR)
    rs2(PS)
    back(col_r, ne_g, tile_g, act_d, split(dot3(d_agg_s, wt(G2), 1, 1)))
    d_recv_s = split(dot2(incidence(gedge_in, ne_g), (eh[0:ne_g, :], el[0:ne_g, :])))
    store_dw(GR, mesh_s, d_recv_s)
    rs1(GR)
    rs2(G2)
    rs3(P2)
    scatter(gedge_in, ne_g, ng, nh, 128)
    send_buf[3] = dtab[ng:tg, :].reshape(bands, 16, d)
    halo = exchange(3)
    rs2(GR)
    rs3(PR)
    scatter(gedge_in, ne_g, 0, ng, 256)
    rs3(PS)

    def split_dtab(r):
        hi, lo = split(dtab[pl.ds(r, 128), :])
        eh[pl.ds(r, 128), :] = hi
        el[pl.ds(r, 128), :] = lo

    loop(tg, 128, split_dtab)
    b = (eh[0:tg, :], el[0:tg, :])
    for t in range(4):
        cols = slice(t * 128, (t + 1) * 128)
        dw[GS, t] = dot3((gh[0:tg, cols], gl[0:tg, cols]), b, 0, 0).reshape(dw.shape[2:])
    rs1(GS)
    rs3(G2)
    out_mesh[0] = d_mid + dot3(d_recv_s, wt(GR), 1, 1)
    arrived(halo)
    ret = split(land[3].reshape(nh, d))

    def grid_step(r):
        own = dtab[pl.ds(r, 256), :] + dot2(pick_g[:, pl.ds(r, 256)], ret, 0, 0)
        grid_v[pl.ds(r, 256), :] = dot3(split(own), wt(GS), 1, 1)

    rs2(GS)
    rs3(GR)
    loop(ng, 256, grid_step)
    out_copy = pltpu.make_async_copy(grid_v, out_grid.at[0], out_sem)
    out_copy.start()
    rs3(GS)
    for w in (P2, PR, PS, G2, GR, GS):
        rs4(w)
    if fused:
        arrived(gain_copies)
        total = gain_mine[...]
        for o in range(n_all - 1):
            total = total + gain_land[o]
        width = d // n_all
        mine = jnp.zeros((8, width), F32)
        for j in range(n_all):
            mine = jnp.where(flat == j, total[:, j * width : (j + 1) * width], mine)
        out_gain[...] = mine[0:2]
    for c in sends:
        c.wait_send()
    out_copy.wait()


def body(cfg, grid_h, mesh_h, cotangent, weights, gains, g2m_send, m2m_send, g2m_edges, m2m_edges):
    bands, nx, nz, fused = cfg["bands"], cfg["nx"], cfg["nz"], cfg["fused"]
    ng, d = grid_h.shape[1:]
    nm = mesh_h.shape[1]
    ne_g, ne_m = g2m_edges.shape[1], m2m_edges.shape[1]
    nh = bands * 16
    tg, tm = ng + nh, nm + nh
    n_all = nz * nx * 2
    rows = d // n_all
    ne = max(ne_g, ne_m, tg)
    scratch = [
        pltpu.VMEM((ng, d), F32),
        pltpu.VMEM((6, d, d), F32),
        pltpu.VMEM((6, d, d), BF16),
        pltpu.VMEM((6, d, d), BF16),
        pltpu.VMEM((tg, d), BF16),
        pltpu.VMEM((tg, d), BF16),
        pltpu.VMEM((tg + nm, d), BF16),
        pltpu.VMEM((tg + nm, d), BF16),
        pltpu.VMEM((ne_g, 128), jnp.int32),
        pltpu.VMEM((ne_g, 128), jnp.int32),
        pltpu.VMEM((ne_g, d), F32),
        pltpu.VMEM((ne, d), BF16),
        pltpu.VMEM((ne, d), BF16),
        pltpu.VMEM((ne_m, 128), jnp.int32),
        pltpu.VMEM((ne_m, 128), jnp.int32),
        pltpu.VMEM((max(tg, ne_m), d), F32),
        pltpu.VMEM((nh, ng), BF16),
        pltpu.VMEM((nh, nm), BF16),
        pltpu.VMEM((4, bands, 16, d), F32),
        pltpu.VMEM((4, bands, 16, d), F32),
        pltpu.SemaphoreType.DMA((7,)),
        pltpu.SemaphoreType.DMA((4, bands)),
        pltpu.SemaphoreType.DMA((4, bands)),
        pltpu.SemaphoreType.DMA,
    ]
    if fused:
        scratch += [
            pltpu.VMEM((6, nz, nx, 2, rows, d), F32),
            pltpu.VMEM((6, nz, nx, rows, d), F32),
            pltpu.VMEM((6, nx - 1, nz, rows, d), F32),
            pltpu.VMEM((6, nz - 1, rows, d), F32),
            pltpu.VMEM((8, d), F32),
            pltpu.VMEM((n_all - 1, 8, d), F32),
            pltpu.SemaphoreType.DMA((6,)),
            pltpu.SemaphoreType.DMA((6,)),
            pltpu.SemaphoreType.DMA((6, nx - 1)),
            pltpu.SemaphoreType.DMA((6, nx - 1)),
            pltpu.SemaphoreType.DMA((6, nz - 1)),
            pltpu.SemaphoreType.DMA((6, nz - 1)),
            pltpu.SemaphoreType.DMA((n_all - 1,)),
            pltpu.SemaphoreType.DMA((n_all - 1,)),
        ]
        w_shape, gain_shape = (6, rows, d), (2, d // n_all)
    else:
        w_shape, gain_shape = (6, 4, d // 4, d), (2, d)
    vmem = pl.BlockSpec(memory_space=pltpu.VMEM)
    hbm = pl.BlockSpec(memory_space=pl.ANY)
    d_grid, d_mesh, d_w, d_gain = pl.pallas_call(
        functools.partial(kernel, cfg),
        out_shape=(
            jax.ShapeDtypeStruct((1, ng, d), F32),
            jax.ShapeDtypeStruct((1, nm, d), F32),
            jax.ShapeDtypeStruct(w_shape, F32),
            jax.ShapeDtypeStruct(gain_shape, F32),
        ),
        in_specs=[hbm, vmem, vmem, hbm, vmem, vmem, vmem, vmem, vmem],
        out_specs=(hbm, vmem, vmem, vmem),
        scratch_shapes=scratch,
        compiler_params=pltpu.CompilerParams(
            collective_id=0, has_side_effects=True, vmem_limit_bytes=62 * 1024 * 1024
        ),
    )(grid_h, mesh_h, cotangent, weights, gains, g2m_send, m2m_send, g2m_edges, m2m_edges)
    if not fused:
        axes = ("dom", "ens", "rep")
        d_w = lax.psum_scatter(d_w.reshape(6, d, d), axes, scatter_dimension=1, tiled=True)
        d_gain = lax.psum_scatter(d_gain, axes, scatter_dimension=1, tiled=True)
    return d_grid, d_mesh, d_w, d_gain


def solution(mesh):
    nz, nx, nr = mesh.shape["dom"], mesh.shape["ens"], mesh.shape["rep"]
    rows = 512 // (nz * nx * nr)
    cfg = dict(bands=nz * nr, nx=nx, nz=nz, fused=nz == 4 and nx > 1 and rows % 8 == 0)
    return jax.shard_map(
        functools.partial(body, cfg),
        mesh=mesh,
        in_specs=(
            P(("groups", "ens"), ("dom", "rep"), None),
            P(("groups", "ens"), ("dom", "rep"), None),
            P(("groups", "ens"), ("dom", "rep"), None),
            P(),
            P(),
            P(("dom", "rep"), None, None),
            P(("dom", "rep"), None, None),
            P(None, ("dom", "rep")),
            P(None, ("dom", "rep")),
        ),
        out_specs=(
            P(("groups", "ens"), ("dom", "rep"), None),
            P(("groups", "ens"), ("dom", "rep"), None),
            P("groups", ("dom", "ens", "rep"), None),
            P("groups", ("dom", "ens", "rep")),
        ),
        check_vma=False,
    )
```

```python
import functools

import jax
import jax.numpy as jnp
from jax import lax
from jax.experimental import pallas as pl
from jax.experimental.pallas import tpu as pltpu
from jax.sharding import PartitionSpec as P

F32 = jnp.float32
BF16 = jnp.bfloat16
MESH = pl.DeviceIdType.MESH

GS, GR, G2, PS, PR, P2 = range(6)

UNITS = (
    (P2, 0, 2, True),
    (PR, 0, 2, False),
    (PS, 0, 2, False),
    (G2, 0, 2, False),
    (GR, 0, 2, False),
    (GS, 0, 1, False),
    (GS, 1, 2, True),
)


def split(x):
    hi = x.astype(BF16)
    return hi, (x - hi.astype(F32)).astype(BF16)


def dot(a, b, ca, cb):
    return lax.dot_general(a, b, (((ca,), (cb,)), ((), ())), preferred_element_type=F32)


def dot3(a, b, ca=1, cb=0):
    return dot(a[0], b[0], ca, cb) + (dot(a[0], b[1], ca, cb) + dot(a[1], b[0], ca, cb))


def dot2(sel, b, ca=1, cb=0):
    return dot(sel, b[0], ca, cb) + dot(sel, b[1], ca, cb)


def ones(mask):
    return jnp.where(mask, 1.0, 0.0).astype(BF16)


def tile_of(n, largest, unit=128):
    return max(t for t in range(unit, largest + 1, unit) if n % t == 0)


def loop(n, tile, fn):
    if n == tile:
        fn(0)
        return

    def step(i, carry):
        fn(pl.multiple_of(i * tile, tile))
        return carry

    lax.fori_loop(0, n // tile, step, 0)


def norm_stats(agg):
    mean = jnp.mean(agg, axis=-1, keepdims=True)
    cen = agg - mean
    rstd = lax.rsqrt(jnp.mean(cen * cen, axis=-1, keepdims=True) + 1e-05)
    return cen * rstd, rstd


def norm_back(d_out, unit, rstd, gain):
    d_unit = d_out * gain
    m1 = jnp.mean(d_unit, axis=-1, keepdims=True)
    m2 = jnp.mean(d_unit * unit, axis=-1, keepdims=True)
    return rstd * (d_unit - m1 - unit * m2), jnp.sum(d_out * unit, axis=0, keepdims=True)


def kernel(
    cfg,
    grid_in, mesh_in, cot_in, w_in, gains_in, gsend_in, msend_in, gedge_in, medge_in,
    *refs,
):
    bands, nx, nz, fused = cfg["bands"], cfg["nx"], cfg["nz"], cfg["fused"]
    refs = list(refs)
    out_grid, out_mesh, out_w, out_gain = refs[:4]
    refs = refs[4:]
    take = lambda: refs.pop(0)
    grid_v, w_v, wh, wl, gh, gl = take(), take(), take(), take(), take(), take()
    th, tl, col_s, col_r, act_d, eh, el = (take() for _ in range(7))
    mcol_s, mcol_r, dtab = take(), take(), take()
    pick_g, pick_m = take(), take()
    send_buf, land, far_send, far_land = take(), take(), take(), take()
    load_sem, halo_ss, halo_rs, out_sem = take(), take(), take(), take()
    if fused:
        dw, r1, r2, r3, r4, gain_mine, gain_land = (take() for _ in range(7))
        rs_ss, rs_rs, gss, gsr = (take() for _ in range(4))
    else:
        dw = out_w

    dom, ens, rep = lax.axis_index("dom"), lax.axis_index("ens"), lax.axis_index("rep")
    me = dom * 2 + rep
    ng, d = grid_v.shape
    nm = mesh_in.shape[1]
    ne_g, ne_m = gedge_in.shape[1], medge_in.shape[1]
    nh = bands * 16
    tg, tm = ng + nh, nm + nh
    flat = (dom * nx + ens) * 2 + rep
    n_all = nz * nx * 2

    def band_id(b):
        return {"dom": b // 2, "rep": lax.rem(b, 2)}

    def flat_id(f):
        return {"dom": f // (2 * nx), "ens": lax.rem(f // 2, nx), "rep": lax.rem(f, 2)}

    loads = [pltpu.make_async_copy(grid_in.at[0], grid_v, load_sem.at[6])]
    loads[0].start()
    w_loads = {}
    for w in (GS, GR, G2, PS, PR, P2):
        w_loads[w] = pltpu.make_async_copy(w_in.at[w], w_v.at[w], load_sem.at[w])
        w_loads[w].start()

    barrier = pltpu.get_barrier_semaphore()
    if fused:
        for o in range(1, n_all):
            pl.semaphore_signal(barrier, inc=1, device_id=flat_id(lax.rem(flat + o, n_all)), device_id_type=MESH)
    else:
        for o in range(1, bands):
            pl.semaphore_signal(barrier, inc=1, device_id=band_id(lax.rem(me + o, bands)), device_id_type=MESH)

    for ph in range(4):
        for o in [0] + list(range(2, bands - 1)):
            land[ph, lax.rem(me + bands - o, bands)] = jnp.zeros((16, d), F32)

    def pick_matrix(send, rows):
        s = send[0]
        wide = jnp.broadcast_to(s[:, None, :], (bands, 16, 16)).reshape(nh, 16)
        slot = lax.rem(lax.broadcasted_iota(jnp.int32, (nh, 16), 0), 16)
        lane = lax.broadcasted_iota(jnp.int32, (nh, 16), 1)
        col = jnp.sum(jnp.where(slot == lane, wide, 0).astype(F32), axis=1, keepdims=True)
        return ones(col.astype(jnp.int32) == lax.broadcasted_iota(jnp.int32, (nh, rows), 1))

    pick_g[...] = pick_matrix(gsend_in, ng)
    pick_m[...] = pick_matrix(msend_in, nm)

    def columns(edges, dst_s, dst_r, n):
        for i in range(n // 128):
            for row, dst in ((0, dst_s), (1, dst_r)):
                line = edges[row : row + 1, i * 128 : (i + 1) * 128]
                dst[i * 128 : (i + 1) * 128, :] = jnp.broadcast_to(line.astype(F32), (128, 128)).T.astype(jnp.int32)

    quarter = d // 4
    near = [o for o in (1, bands - 1)]
    far = list(range(2, bands - 1))

    def exchange(ph):
        copies = []
        for o in near + far:
            to = lax.rem(me + o, bands)
            if o in near:
                src, dst = send_buf.at[ph, to], land.at[ph, me]
            else:
                for k in range(2):
                    for c in range(4):
                        far_send[ph, to, 4 * k + c : 4 * k + c + 1, :] = send_buf[
                            ph, to, k : k + 1, c * quarter : (c + 1) * quarter
                        ]
                src, dst = far_send.at[ph, to], far_land.at[ph, me]
            c = pltpu.make_async_remote_copy(
                src_ref=src,
                dst_ref=dst,
                send_sem=halo_ss.at[ph, o],
                recv_sem=halo_rs.at[ph, o],
                device_id=band_id(to),
                device_id_type=MESH,
            )
            c.start()
            copies.append(c)
        return copies

    sends = []

    def arrived(copies):
        for c in copies:
            c.wait_recv()
        sends.extend(copies)

    def halo_arrived(ph, copies):
        arrived(copies)
        for o in far:
            src = lax.rem(me + bands - o, bands)
            for k in range(2):
                for c in range(4):
                    land[ph, src, k : k + 1, c * quarter : (c + 1) * quarter] = far_land[
                        ph, src, 4 * k + c : 4 * k + c + 1, :
                    ]
        return land[ph].reshape(nh, d)

    loads[0].wait()

    def split_grid(r):
        hi, lo = split(grid_v[pl.ds(r, 256), :])
        gh[pl.ds(r, 256), :] = hi
        gl[pl.ds(r, 256), :] = lo

    loop(ng, 256, split_grid)
    send_buf[0] = dot2(pick_g[...], (gh[0:ng, :], gl[0:ng, :])).reshape(bands, 16, d)
    pl.semaphore_wait(barrier, (n_all if fused else bands) - 1)
    halo = exchange(0)

    def load_w(w):
        w_loads[w].wait()
        hi, lo = split(w_v[w])
        wh[w] = hi
        wl[w] = lo

    def wt(w):
        return wh[w], wl[w]

    def put_table(r, value):
        hi, lo = split(value)
        n = value.shape[0]
        th[pl.ds(r, n), :] = hi
        tl[pl.ds(r, n), :] = lo

    load_w(GS)

    def project(r):
        put_table(r, dot3((gh[pl.ds(r, 256), :], gl[pl.ds(r, 256), :]), wt(GS)))

    loop(ng, 256, project)
    load_w(GR)
    mesh = mesh_in[0]
    mesh_s = split(mesh)
    put_table(tg, dot3(mesh_s, wt(GR)))
    columns(gedge_in, col_s, col_r, ne_g)
    columns(medge_in, mcol_s, mcol_r, ne_m)
    load_w(G2)
    load_w(PS)
    load_w(PR)
    load_w(P2)
    hi, lo = split(halo_arrived(0, halo))
    gh[ng:tg, :] = hi
    gl[ng:tg, :] = lo
    put_table(ng, dot3((hi, lo), wt(GS)))

    def gather(cs, cr, ne, table, tile, act):
        total = table + nm

        def step(r):
            s = cs[pl.ds(r, tile), :]
            t = cr[pl.ds(r, tile), :]
            lane = lax.broadcasted_iota(jnp.int32, (tile, 128), 1)
            parts = [ones(s == lane + j * 128) for j in range(table // 128)] + [ones(t == lane)]
            sel = jnp.concatenate(parts, axis=1)
            pre = dot2(sel, (th[0:total, :], tl[0:total, :]))
            sig = jax.nn.sigmoid(pre)
            hidden = pre * sig
            act[pl.ds(r, tile), :] = sig + hidden * (1.0 - sig)
            h, l = split(hidden)
            eh[pl.ds(r, tile), :] = h
            el[pl.ds(r, tile), :] = l

        loop(ne, tile, step)

    def incidence(edges, ne):
        return ones(edges[1:2, :] == lax.broadcasted_iota(jnp.int32, (nm, ne), 0))

    def back(cr, ne, tile, act, ds):
        def step(r):
            sel = ones(cr[pl.ds(r, tile), :] == lax.broadcasted_iota(jnp.int32, (tile, 128), 1))
            h, l = split(dot2(sel, ds) * act[pl.ds(r, tile), :])
            eh[pl.ds(r, tile), :] = h
            el[pl.ds(r, tile), :] = l

        loop(ne, tile, step)

    def scatter(edges, ne, first, n, tile):
        def step(r):
            node = lax.broadcasted_iota(jnp.int32, (tile, ne), 0) + (first + r)
            dtab[pl.ds(first + r, tile), :] = dot2(ones(edges[0:1, :] == node), (eh[0:ne, :], el[0:ne, :]))

        loop(n, tile, step)

    def put_dw(w, t, value):
        if not fused:
            dw[w, t] = value
            return
        n = dw.shape[4]
        for x in range(2):
            for c in range(2):
                dw[w, c, t, x] = value[(2 * x + c) * n : (2 * x + c + 1) * n]

    def store_dw(w, a, b):
        for t in range(4):
            cols = slice(t * 128, (t + 1) * 128)
            put_dw(w, t, dot3((a[0][:, cols], a[1][:, cols]), b, 0, 0))

    z_hi, z_lo = dom // 2, lax.rem(dom, 2)
    rs_copies = {}

    def rs_start(u, stage, pairs, device_id):
        rs_copies[u] = []
        for i, (src, dst) in enumerate(pairs):
            c = pltpu.make_async_remote_copy(
                src_ref=src, dst_ref=dst, send_sem=rs_ss.at[u, stage, i], recv_sem=rs_rs.at[u, stage, i],
                device_id=device_id, device_id_type=MESH,
            )
            c.start()
            rs_copies[u].append(c)

    def rs(u, stage):
        if not fused:
            return
        w, lo, hi, z_first = UNITS[u]
        half = out_w.shape[1] // 2
        rows = slice(lo * half, hi * half)
        if stage > 0:
            arrived(rs_copies[u])
        to_x = {"ens": 1 - ens}
        to_z = {"dom": 2 * z_hi + (1 - z_lo)}
        to_far = {"dom": 2 * (1 - z_hi) + z_lo}
        if stage == 0:
            rs_start(u, 0, [(dw.at[w, 1 - rep, :, :, rows], r1.at[w, :, :, rows])], {"rep": 1 - rep})
        elif stage == 1:
            r1[w, :, :, rows] = r1[w, :, :, rows] + dw[w, rep, :, :, rows]
            if z_first:
                pairs = [(r1.at[w, 2 * p + 1 - z_lo, :, rows], r2.at[w, 2 * p : 2 * p + 2, rows]) for p in range(2)]
                rs_start(u, 1, pairs, to_z)
            else:
                rs_start(u, 1, [(r1.at[w, :, 1 - ens, rows], r2.at[w, :, rows])], to_x)
        elif stage == 2:
            if z_first:
                for p in range(2):
                    both = slice(2 * p, 2 * p + 2)
                    r2[w, both, rows] = r2[w, both, rows] + r1[w, 2 * p + z_lo, :, rows]
                rs_start(u, 2, [(r2.at[w, pl.ds(2 * (1 - z_hi), 2), rows], r3.at[w, :, rows])], to_far)
            else:
                r2[w, :, rows] = r2[w, :, rows] + r1[w, :, ens, rows]
                rs_start(u, 2, [(r2.at[w, 2 * p + 1 - z_lo, rows], r3.at[w, p, rows]) for p in range(2)], to_z)
        elif stage == 3:
            for p in range(2):
                own = r2[w, 2 * z_hi + p, rows] if z_first else r2[w, 2 * p + z_lo, rows]
                r3[w, p, rows] = r3[w, p, rows] + own
            if z_first:
                rs_start(u, 3, [(r3.at[w, 1 - ens, rows], r4.at[w, rows])], to_x)
            else:
                rs_start(u, 3, [(r3.at[w, 1 - z_hi, rows], r4.at[w, rows])], to_far)
        else:
            own = r3[w, ens, rows] if z_first else r3[w, z_hi, rows]
            out_w[w, rows] = r4[w, rows] + own

    tile_g = ne_g // 4 if (ne_g // 4) % 16 == 0 else 128
    tile_m = tile_of(ne_m, 512)
    gather(col_s, col_r, ne_g, tg, tile_g, act_d)
    sum_g = split(dot2(incidence(gedge_in, ne_g), (eh[0:ne_g, :], el[0:ne_g, :])))
    unit_g, rstd_g = norm_stats(dot3(sum_g, wt(G2)))
    mid = mesh + unit_g * gains_in[0:1, :]
    mid_s = split(mid)

    send_buf[1] = dot2(pick_m[...], mid_s).reshape(bands, 16, d)
    halo = exchange(1)
    put_table(0, dot3(mid_s, wt(PS)))
    put_table(tm, dot3(mid_s, wt(PR)))
    halo_s = split(halo_arrived(1, halo))
    put_table(nm, dot3(halo_s, wt(PS)))
    act_m = dtab
    gather(mcol_s, mcol_r, ne_m, tm, tile_m, act_m)
    sum_m = split(dot2(incidence(medge_in, ne_m), (eh[0:ne_m, :], el[0:ne_m, :])))
    unit_m, rstd_m = norm_stats(dot3(sum_m, wt(P2)))

    cot = cot_in[0]
    d_agg, d_gain_p = norm_back(cot, unit_m, rstd_m, gains_in[1:2, :])
    d_agg_s = split(d_agg)
    back(mcol_r, ne_m, tile_m, act_m, split(dot3(d_agg_s, wt(P2), 1, 1)))
    scatter(medge_in, ne_m, 0, tm, tile_of(tm, 384))
    send_buf[2] = dtab[nm:tm, :].reshape(bands, 16, d)
    halo = exchange(2)
    store_dw(P2, sum_m, d_agg_s)
    rs(0, 0)
    d_recv_s = split(dot2(incidence(medge_in, ne_m), (eh[0:ne_m, :], el[0:ne_m, :])))
    store_dw(PR, mid_s, d_recv_s)
    rs(1, 0)
    rs(0, 1)
    both = [jnp.concatenate([a, b], axis=0) for a, b in zip(mid_s, halo_s)]
    store_dw(PS, both, split(dtab[0:tm, :]))
    rs(2, 0)
    rs(1, 1)
    d_mid = cot + dot3(d_recv_s, wt(PR), 1, 1)
    own = dtab[0:nm, :] + dot2(pick_m[...], split(halo_arrived(2, halo)), 0, 0)
    rs(2, 1)
    d_mid = d_mid + dot3(split(own), wt(PS), 1, 1)

    d_agg, d_gain_g = norm_back(d_mid, unit_g, rstd_g, gains_in[0:1, :])
    if fused:
        row = lax.broadcasted_iota(jnp.int32, (8, quarter), 0)
        packed = jnp.zeros((8, quarter), F32)
        for g, gain in enumerate((d_gain_g, d_gain_p)):
            full = jnp.broadcast_to(gain, (8, d))
            for c in range(4):
                packed = jnp.where(row == 4 * g + c, full[:, c * quarter : (c + 1) * quarter], packed)
        gain_mine[...] = packed
        gain_copies = []
        for o in range(1, n_all):
            c = pltpu.make_async_remote_copy(
                src_ref=gain_mine, dst_ref=gain_land.at[o - 1], send_sem=gss.at[o - 1], recv_sem=gsr.at[o - 1],
                device_id=flat_id(lax.rem(flat + o, n_all)), device_id_type=MESH,
            )
            c.start()
            gain_copies.append(c)
    else:
        out_gain[0:1, :] = d_gain_g
        out_gain[1:2, :] = d_gain_p
    d_agg_s = split(d_agg)
    store_dw(G2, sum_g, d_agg_s)
    rs(3, 0)
    back(col_r, ne_g, tile_g, act_d, split(dot3(d_agg_s, wt(G2), 1, 1)))
    rs(0, 2)
    rs(3, 1)
    rs(1, 2)
    d_recv_s = split(dot2(incidence(gedge_in, ne_g), (eh[0:ne_g, :], el[0:ne_g, :])))
    store_dw(GR, mesh_s, d_recv_s)
    rs(4, 0)
    scatter(gedge_in, ne_g, ng, nh, 128)
    send_buf[3] = dtab[ng:tg, :].reshape(bands, 16, d)
    halo = exchange(3)
    rs(4, 1)
    rs(0, 3)
    scatter(gedge_in, ne_g, 0, ng // 2, 256)
    rs(2, 2)
    rs(1, 3)
    scatter(gedge_in, ne_g, ng // 2, ng // 2, 256)

    def split_dtab(r):
        hi, lo = split(dtab[pl.ds(r, 128), :])
        eh[pl.ds(r, 128), :] = hi
        el[pl.ds(r, 128), :] = lo

    loop(tg, 128, split_dtab)
    b = (eh[0:tg, :], el[0:tg, :])
    for t in range(4):
        cols = slice(t * 128, (t + 1) * 128)
        put_dw(GS, t, dot3((gh[0:tg, cols], gl[0:tg, cols]), b, 0, 0))
    rs(6, 0)
    rs(5, 0)
    rs(2, 3)
    out_mesh[0] = d_mid + dot3(d_recv_s, wt(GR), 1, 1)
    rs(6, 1)
    rs(5, 1)
    rs(3, 2)
    ret = split(halo_arrived(3, halo))

    def grid_step(r):
        own = dtab[pl.ds(r, 256), :] + dot2(pick_g[:, pl.ds(r, 256)], ret, 0, 0)
        grid_v[pl.ds(r, 256), :] = dot3(split(own), wt(GS), 1, 1)

    loop(ng // 2, 256, grid_step)
    rs(3, 3)
    rs(4, 2)
    loop(ng // 2, 256, lambda r: grid_step(r + ng // 2))
    out_copy = pltpu.make_async_copy(grid_v, out_grid.at[0], out_sem)
    out_copy.start()
    for u in (0, 1, 2):
        rs(u, 4)
    rs(6, 2)
    rs(4, 3)
    rs(5, 2)
    rs(6, 3)
    rs(5, 3)
    if fused:
        arrived(gain_copies)
        total = gain_mine[...]
        for o in range(n_all - 1):
            total = total + gain_land[o]
        width = d // n_all
        per = quarter // width
        row = lax.broadcasted_iota(jnp.int32, (8, quarter), 0)
        line = [
            jnp.sum(jnp.where(row == 4 * g + flat // per, total, 0.0), axis=0, keepdims=True) for g in range(2)
        ]
        wide = jnp.where(row == 0, line[0], jnp.where(row == 1, line[1], 0.0))
        mine = jnp.zeros((8, width), F32)
        for j in range(per):
            mine = jnp.where(lax.rem(flat, per) == j, wide[:, j * width : (j + 1) * width], mine)
        out_gain[...] = mine[0:2]
    for u in (3, 4, 6, 5):
        rs(u, 4)
    for c in sends:
        c.wait_send()
    out_copy.wait()


def body(cfg, grid_h, mesh_h, cotangent, weights, gains, g2m_send, m2m_send, g2m_edges, m2m_edges):
    bands, nx, nz, fused = cfg["bands"], cfg["nx"], cfg["nz"], cfg["fused"]
    ng, d = grid_h.shape[1:]
    nm = mesh_h.shape[1]
    ne_g, ne_m = g2m_edges.shape[1], m2m_edges.shape[1]
    nh = bands * 16
    tg, tm = ng + nh, nm + nh
    n_all = nz * nx * 2
    rows = d // n_all
    ne = max(ne_g, ne_m, tg)
    scratch = [
        pltpu.VMEM((ng, d), F32),
        pltpu.VMEM((6, d, d), F32),
        pltpu.VMEM((6, d, d), BF16),
        pltpu.VMEM((6, d, d), BF16),
        pltpu.VMEM((tg, d), BF16),
        pltpu.VMEM((tg, d), BF16),
        pltpu.VMEM((tg + nm, d), BF16),
        pltpu.VMEM((tg + nm, d), BF16),
        pltpu.VMEM((ne_g, 128), jnp.int32),
        pltpu.VMEM((ne_g, 128), jnp.int32),
        pltpu.VMEM((ne_g, d), F32),
        pltpu.VMEM((ne, d), BF16),
        pltpu.VMEM((ne, d), BF16),
        pltpu.VMEM((ne_m, 128), jnp.int32),
        pltpu.VMEM((ne_m, 128), jnp.int32),
        pltpu.VMEM((max(tg, ne_m), d), F32),
        pltpu.VMEM((nh, ng), BF16),
        pltpu.VMEM((nh, nm), BF16),
        pltpu.VMEM((4, bands, 16, d), F32),
        pltpu.VMEM((4, bands, 16, d), F32),
        pltpu.VMEM((4, bands, 8, d // 4), F32),
        pltpu.VMEM((4, bands, 8, d // 4), F32),
        pltpu.SemaphoreType.DMA((7,)),
        pltpu.SemaphoreType.DMA((4, bands)),
        pltpu.SemaphoreType.DMA((4, bands)),
        pltpu.SemaphoreType.DMA,
    ]
    if fused:
        scratch += [
            pltpu.VMEM((6, 2, 4, 2, rows, d), F32),
            pltpu.VMEM((6, 4, 2, rows, d), F32),
            pltpu.VMEM((6, 4, rows, d), F32),
            pltpu.VMEM((6, 2, rows, d), F32),
            pltpu.VMEM((6, rows, d), F32),
            pltpu.VMEM((8, d // 4), F32),
            pltpu.VMEM((n_all - 1, 8, d // 4), F32),
            pltpu.SemaphoreType.DMA((len(UNITS), 4, 2)),
            pltpu.SemaphoreType.DMA((len(UNITS), 4, 2)),
            pltpu.SemaphoreType.DMA((n_all - 1,)),
            pltpu.SemaphoreType.DMA((n_all - 1,)),
        ]
        w_shape, gain_shape = (6, rows, d), (2, d // n_all)
    else:
        w_shape, gain_shape = (6, 4, d // 4, d), (2, d)
    vmem = pl.BlockSpec(memory_space=pltpu.VMEM)
    hbm = pl.BlockSpec(memory_space=pl.ANY)
    d_grid, d_mesh, d_w, d_gain = pl.pallas_call(
        functools.partial(kernel, cfg),
        out_shape=(
            jax.ShapeDtypeStruct((1, ng, d), F32),
            jax.ShapeDtypeStruct((1, nm, d), F32),
            jax.ShapeDtypeStruct(w_shape, F32),
            jax.ShapeDtypeStruct(gain_shape, F32),
        ),
        in_specs=[hbm, vmem, vmem, hbm, vmem, vmem, vmem, vmem, vmem],
        out_specs=(hbm, vmem, vmem, vmem),
        scratch_shapes=scratch,
        compiler_params=pltpu.CompilerParams(
            collective_id=0, has_side_effects=True, vmem_limit_bytes=62 * 1024 * 1024
        ),
    )(grid_h, mesh_h, cotangent, weights, gains, g2m_send, m2m_send, g2m_edges, m2m_edges)
    if not fused:
        axes = ("dom", "ens", "rep")
        d_w = lax.psum_scatter(d_w.reshape(6, d, d), axes, scatter_dimension=1, tiled=True)
        d_gain = lax.psum_scatter(d_gain, axes, scatter_dimension=1, tiled=True)
    return d_grid, d_mesh, d_w, d_gain


def solution(mesh):
    nz, nx, nr = mesh.shape["dom"], mesh.shape["ens"], mesh.shape["rep"]
    rows = 512 // (nz * nx * nr)
    cfg = dict(bands=nz * nr, nx=nx, nz=nz, fused=nz == 4 and nx == 2 and rows % 16 == 0)
    return jax.shard_map(
        functools.partial(body, cfg),
        mesh=mesh,
        in_specs=(
            P(("groups", "ens"), ("dom", "rep"), None),
            P(("groups", "ens"), ("dom", "rep"), None),
            P(("groups", "ens"), ("dom", "rep"), None),
            P(),
            P(),
            P(("dom", "rep"), None, None),
            P(("dom", "rep"), None, None),
            P(None, ("dom", "rep")),
            P(None, ("dom", "rep")),
        ),
        out_specs=(
            P(("groups", "ens"), ("dom", "rep"), None),
            P(("groups", "ens"), ("dom", "rep"), None),
            P("groups", ("dom", "ens", "rep"), None),
            P("groups", ("dom", "ens", "rep")),
        ),
        check_vma=False,
    )
```
